32 devices in a mesh: seg: 8 (over z, y), head: 4 (over x, core).
Axes of the slice: x: 2, y: 2, z: 4, core: 2. Of those that a mesh axis runs over, the one named last changes fastest.
Arguments:
- inputs: bfloat16 [16, 512, 1024], P('seg', None, 'head'), may hold values from -0.25 to 0.25
- cotangent: bfloat16 [16, 512, 1024], P('seg', None, 'head'), may hold values from -0.25 to 0.25
- state_in: bfloat16 [16, 512, 128], P('seg'), may hold values from -1.75 to 1.75
- state_out: bfloat16 [16, 512, 128], P('seg'), may hold values from -1.75 to 1.75
- log_decay: float32 [16, 16, 512], P('seg', 'head'), may hold values from -1 to 0
- parents: int32 [16], replicated, may hold values from -1 to 7, as said below
- slot_segment: int32 [16], replicated, may hold values from 0 to 15, as said below
Outputs:
- grad_inputs: bfloat16 [16, 512, 1024], P('seg', None, 'head')
- grad_state_in: float32 [16, 512, 128], P('seg', 'head')
- grad_state_out: float32 [16, 512, 128], P('seg', 'head')
The draws below stay inside these ranges and needn't reach their ends.
Inputs may be any that keep to these rules, and one draw needn't show every extreme that they name: parents[s] is -1 for s < 2; each of the next 6 segments has a parent below 2; every other segment has a parent from 2 to 7; every segment below 8 has a child. `slot_segment`: each segment is held in exactly one slot.
All inputs are finite; a program needn't handle non-finite values.
Results may differ from the reference program's by a relative error of at most 0.0085.
Values sent between devices are 32-bit elements; how exact they have to be, the bound alone decides.
No kernel may reach another device: no remote copies, remote signals or barrier semaphores. Data moves between devices by JAX's collectives and lax.ppermute only.
A program may use at most 64 MiB of HBM per device.

```python
import math
import jax
import jax.numpy as jnp
from jax import lax

HEAD_DIM = 64
STATE = 128
HEADS = 16
PIECE_POSITIONS = 512
SEG_DEV = 2
SEGS = 16
ROOTS = 2
MIDS = 6


def draw_log_decay(key, part):
    key = jax.random.fold_in(key, 5)
    sampler_seeds = jax.random.split(key, 6)
    grid_extents = (SEGS, HEADS, PIECE_POSITIONS)
    slow = jnp.exp(jax.random.uniform(sampler_seeds[0], (SEGS, HEADS, 1), jnp.float32, math.log(0.3), math.log(1.2))) / (3.0 * PIECE_POSITIONS)
    fast = jnp.exp(jax.random.uniform(sampler_seeds[1], (SEGS, HEADS, 1), jnp.float32, math.log(1.0 / 50.0), math.log(1.0 / 30.0)))
    share = 0.5
    quick = jax.random.uniform(sampler_seeds[2], (SEGS, HEADS, 1), jnp.float32) < share
    forgetting_factor = jnp.where(quick, fast, slow)
    approximate_guess = jax.random.uniform(sampler_seeds[3], grid_extents, jnp.float32, 0.5, 2.0)
    span_count = (jax.random.uniform(sampler_seeds[4], grid_extents, jnp.float32) < 0.5 / PIECE_POSITIONS).astype(jnp.float32)
    hierarchy_levels = jax.random.uniform(sampler_seeds[5], grid_extents, jnp.float32, 0.22, 0.69)
    return -(forgetting_factor * approximate_guess + span_count * hierarchy_levels)


def draw_parents(key, part):
    key = jax.random.fold_in(key, 11)
    sampler_seeds = jax.random.split(key, 3)
    index = jnp.arange(SEGS, dtype=jnp.int32)
    mid_random = jax.random.randint(sampler_seeds[0], (SEGS,), 0, ROOTS, jnp.int32)
    mid_offset = index - ROOTS
    mid_parent = jnp.where(mid_offset < 3, 0, jnp.where(mid_offset < ROOTS + 2, mid_offset - 2, mid_random))
    leaf_first = jax.random.randint(sampler_seeds[1], (SEGS,), 0, MIDS, jnp.int32)
    leaf_second = jax.random.randint(sampler_seeds[2], (SEGS,), 0, MIDS, jnp.int32)
    leaf_offset = index - ROOTS - MIDS
    leaf_parent = ROOTS + jnp.where(leaf_offset < MIDS, jnp.maximum(leaf_offset, 0) % MIDS, jnp.minimum(leaf_first, leaf_second))
    result = jnp.where(index < ROOTS, -1, jnp.where(index < ROOTS + MIDS, mid_parent, leaf_parent))
    return result.astype(jnp.int32)


def place_segment(order, segment_id, slot):
    everyone = jnp.arange(SEGS, dtype=jnp.int32)
    where_now = jnp.sum(jnp.where(order == segment_id, everyone, 0)).astype(jnp.int32)
    occupant = order[slot]
    order = order.at[where_now].set(occupant)
    return order.at[slot].set(segment_id)


def draw_slot_segment(key, part):
    key = jax.random.fold_in(key, 17)
    sampler_seeds = jax.random.split(key, 3)
    device_count = SEGS // SEG_DEV
    order = jax.random.permutation(sampler_seeds[0], jnp.arange(SEGS, dtype=jnp.int32)).astype(jnp.int32)
    anchor = jax.random.randint(sampler_seeds[1], (), 0, device_count, jnp.int32)
    offsets = jax.random.randint(sampler_seeds[2], (4,), 0, SEG_DEV, jnp.int32)
    devices = jnp.stack([anchor, (anchor + device_count - 1) % device_count, (anchor + device_count // 2) % device_count, (anchor + 1) % device_count]).astype(jnp.int32)
    slots = (devices * SEG_DEV + offsets).astype(jnp.int32)
    order = place_segment(order, 0, slots[0])
    order = place_segment(order, ROOTS, slots[1])
    order = place_segment(order, ROOTS + 1, slots[2])
    order = place_segment(order, ROOTS + 2, slots[3])
    return order.astype(jnp.int32)


def steps_of(stream_key, extent, shards, smallest, high):
    gain, own = 1.0, jax.random.fold_in(stream_key, 6)
    for dim, shards_of in shards:
        heights = jnp.exp(jax.random.uniform(jax.random.fold_in(own, dim), (shards_of,), jnp.float32, smallest / len(shards), high / len(shards)))
        gain = gain * jnp.repeat(heights, extent[dim] // shards_of).reshape([-1 if axis == dim else 1 for axis in range(len(extent))])
    return gain


def centred(rng, shape, width, most, cuts=(), held_as=jnp.bfloat16):
    drawn = jax.random.normal(rng, shape, jnp.float32) * width
    if len(cuts) > 0:
        drawn = steps_of(rng, shape, cuts, -0.22, 0.18) * drawn
    return jnp.clip(drawn, min=-most, max=most).astype(held_as)


def setup_inputs(seed: int = 0) -> dict:
    keys = jax.random.split(jax.random.key(seed), 8)
    return {
        "inputs": centred(keys[0], (SEGS, PIECE_POSITIONS, HEADS * HEAD_DIM), (PIECE_POSITIONS ** -0.5), 0.25, ((0, 8), (2, 4))),
        "cotangent": centred(keys[1], (SEGS, PIECE_POSITIONS, HEADS * HEAD_DIM), (PIECE_POSITIONS ** -0.5), 0.25, ((0, 8), (2, 4))),
        "state_in": centred(keys[2], (SEGS, PIECE_POSITIONS, STATE), (STATE ** -0.25), 1.75, ((0, 8),)),
        "state_out": centred(keys[3], (SEGS, PIECE_POSITIONS, STATE), (STATE ** -0.25), 1.75, ((0, 8),)),
        "log_decay": draw_log_decay(jax.random.fold_in(keys[7], 71), 0),
        "parents": draw_parents(jax.random.fold_in(keys[7], 71), 0),
        "slot_segment": draw_slot_segment(jax.random.fold_in(keys[7], 71), 0),
    }


def causal_decay(cumulative):
    length = cumulative.shape[1]
    later = jnp.arange(length)[:, None] >= jnp.arange(length)[None, :]
    spread = cumulative[:, :, None] - cumulative[:, None, :]
    return jnp.where(later[None], jnp.exp(jnp.where(later[None], spread, 0.0)), 0.0)


def segment_local(sliced):
    inputs_s, cotan_s, sin_s, sout_s, decay_s = sliced
    length = inputs_s.shape[0]
    head_count = decay_s.shape[0]
    head_width = inputs_s.shape[1] // head_count
    cumulative = jnp.cumsum(decay_s, axis=1)
    to_end = jnp.exp(cumulative[:, -1:] - cumulative)
    from_start = jnp.exp(cumulative)
    input_heads = inputs_s.reshape(length, head_count, head_width).astype(jnp.float32)
    cotan_heads = cotan_s.reshape(length, head_count, head_width).astype(jnp.float32)
    scaled_in = (input_heads * to_end.T[:, :, None]).astype(jnp.bfloat16)
    scaled_cot = (cotan_heads * from_start.T[:, :, None]).astype(jnp.bfloat16)
    local_end = jnp.einsum("lhp,ln->hpn", scaled_in.astype(jnp.float32), sin_s.astype(jnp.float32))
    local_adj = jnp.einsum("lhp,ln->hpn", scaled_cot.astype(jnp.float32), sout_s.astype(jnp.float32))
    return local_end, local_adj, jnp.exp(cumulative[:, -1])


def segment_grads(sliced):
    inputs_s, cotan_s, sin_s, sout_s, decay_s, start_state, adjoint_end = sliced
    length = inputs_s.shape[0]
    head_count = decay_s.shape[0]
    head_width = inputs_s.shape[1] // head_count
    cumulative = jnp.cumsum(decay_s, axis=1)
    to_end = jnp.exp(cumulative[:, -1:] - cumulative)
    from_start = jnp.exp(cumulative)
    input_heads = inputs_s.reshape(length, head_count, head_width).astype(jnp.float32)
    cotan_heads = cotan_s.reshape(length, head_count, head_width).astype(jnp.float32)
    sin_full = sin_s.astype(jnp.float32)
    sout_full = sout_s.astype(jnp.float32)
    scores = jnp.dot(sout_s, sin_s.T, preferred_element_type=jnp.float32)
    decay_mask = causal_decay(cumulative)
    weights = (decay_mask * scores[None]).astype(jnp.bfloat16)
    quad_in = jnp.einsum("htu,thp->uhp", weights.astype(jnp.float32), cotan_heads)
    state_in_term = to_end.T[:, :, None] * jnp.einsum("un,hpn->uhp", sin_full, adjoint_end, precision=lax.Precision.HIGHEST)
    grad_in = (quad_in + state_in_term).astype(jnp.bfloat16).reshape(length, head_count * head_width)
    products = jnp.einsum("thp,uhp->htu", cotan_heads, input_heads)
    coupled = (decay_mask * products).astype(jnp.bfloat16).astype(jnp.float32)
    write_quad = jnp.einsum("htu,tn->un", coupled, sout_full)
    read_quad = jnp.einsum("htu,un->tn", coupled, sin_full)
    write_state = jnp.sum(to_end.T[:, :, None] * jnp.einsum("uhp,hpn->uhn", input_heads, adjoint_end, precision=lax.Precision.HIGHEST), axis=1)
    read_state = jnp.sum(from_start.T[:, :, None] * jnp.einsum("thp,hpn->thn", cotan_heads, start_state, precision=lax.Precision.HIGHEST), axis=1)
    return grad_in, write_quad + write_state, read_quad + read_state


def reference(inputs, cotangent, state_in, state_out, log_decay, parents, slot_segment):
    slot_count = inputs.shape[0]
    local_end, local_adj, end_decay = lax.map(segment_local, (inputs, cotangent, state_in, state_out, log_decay))
    position = jnp.zeros((slot_count,), jnp.int32).at[slot_segment].set(jnp.arange(slot_count, dtype=jnp.int32))
    end_seg = local_end[position]
    adj_seg = local_adj[position]
    decay_seg = end_decay[position][:, :, None, None]
    has_parent = (parents >= 0)[:, None, None, None]
    safe_parent = jnp.maximum(parents, 0).astype(jnp.int32)
    start_seg = jnp.zeros_like(end_seg)
    for sweep in range(2):
        end_states = decay_seg * start_seg + end_seg
        start_seg = jnp.where(has_parent, end_states[safe_parent], 0.0)
    target = jnp.where(parents >= 0, parents, slot_count).astype(jnp.int32)
    adjoint_seg = jnp.zeros_like(adj_seg)
    for sweep in range(2):
        begin_adj = adj_seg + decay_seg * adjoint_seg
        adjoint_seg = jax.ops.segment_sum(begin_adj, target, num_segments=slot_count + 1)[:slot_count]
    start_slot = start_seg[slot_segment]
    adjoint_slot = adjoint_seg[slot_segment]
    grad_inputs, grad_state_in, grad_state_out = lax.map(segment_grads, (inputs, cotangent, state_in, state_out, log_decay, start_slot, adjoint_slot))
    return grad_inputs, grad_state_in, grad_state_out
```

```python
import functools

import jax
import jax.numpy as jnp
from jax import lax
from jax.experimental import pallas as pl
from jax.experimental.pallas import tpu as pltpu
from jax.sharding import PartitionSpec as P

ROOTS = 2
MIDS = 6
PARENTS = ROOTS + MIDS
BLOCK = 128
F32 = jnp.float32
BF16 = jnp.bfloat16


def dot(a, b, dims):
    return lax.dot_general(a, b, (dims, ((), ())), preferred_element_type=F32)


NN = ((1,), (0,))
NT = ((1,), (1,))
TN = ((0,), (0,))


def two_parts(x):
    upper = x.astype(BF16).astype(F32)
    return jnp.concatenate([upper, x - upper], axis=0).astype(BF16)


def head_columns(rows, seg, heads, width):
    row = lax.broadcasted_iota(jnp.int32, (2 * rows, width), 0) % rows
    col = lax.broadcasted_iota(jnp.int32, (2 * rows, width), 1) // (width // heads)
    return (row == seg * heads + col).astype(BF16)


def rows_of(chain, order, rel, count):
    me = lax.axis_index("seg")
    first = jnp.bitwise_and(jnp.right_shift(me, order[0]), 1)
    second = jnp.bitwise_and(jnp.right_shift(me, order[1]), 1)
    part = jnp.bitwise_xor(first * 2 + second, rel)
    return pl.multiple_of((chain * 4 + part) * count, count)


def local_kernel(orders, in_hbm, cot_hbm, sin_hbm, sout_hbm, decay_hbm,
                 scin_ref, sccot_ref, cum_ref, toend_ref, decays_ref, *refs):
    states_s, in_ref, cot_ref, sin_ref, sout_ref, decay_ref, sems = refs[-7:]
    copies = [
        pltpu.make_async_copy(src, dst, sems.at[i])
        for i, (src, dst) in enumerate((
            (decay_hbm, decay_ref), (in_hbm, in_ref), (sin_hbm, sin_ref),
            (cot_hbm, cot_ref), (sout_hbm, sout_ref),
        ))
    ]
    for copy in copies:
        copy.start()
    segs, _, width = in_ref.shape
    heads, length = decay_ref.shape[1:]
    rows = segs * heads
    copies[0].wait()
    decay = jnp.concatenate([decay_ref[s] for s in range(segs)], axis=0)
    p0 = decay.astype(BF16).astype(F32)
    r0 = decay - p0
    p1 = r0.astype(BF16).astype(F32)
    pieces = jnp.concatenate([p0, p1, r0 - p1], axis=0).astype(BF16)
    tri = (
        lax.broadcasted_iota(jnp.int32, (BLOCK, BLOCK), 0)
        <= lax.broadcasted_iota(jnp.int32, (BLOCK, BLOCK), 1)
    ).astype(BF16)
    before = jnp.zeros((rows, 1), F32)
    parts = []
    for b in range(length // BLOCK):
        sums = dot(pieces[:, b * BLOCK:(b + 1) * BLOCK], tri, NN)
        part = sums[:rows] + sums[rows:2 * rows] + sums[2 * rows:] + before
        before = part[:, BLOCK - 1:]
        parts.append(part)
    cum = jnp.concatenate(parts, axis=1)
    cum_ref[...] = cum
    row = lax.broadcasted_iota(jnp.int32, (rows, width), 0)
    col = lax.broadcasted_iota(jnp.int32, (rows, width), 1) // (width // heads)
    for s in range(segs):
        of_head = jnp.where(row == s * heads + col, jnp.exp(before), 0.0)
        decays_ref[s:s + 1] = jnp.sum(of_head, axis=0, keepdims=True)
    to_end = two_parts(jnp.exp(before - cum))
    toend_ref[...] = to_end
    from_start = two_parts(jnp.exp(cum))
    for i, (src, scaled_ref, factor, state_ref) in enumerate((
        (in_ref, scin_ref, to_end, sin_ref), (cot_ref, sccot_ref, from_start, sout_ref)
    )):
        copies[2 * i + 1].wait()
        for s in range(segs):
            spread = dot(factor, head_columns(rows, s, heads, width), TN)
            scaled_ref[s] = (src[s].astype(F32) * spread).astype(BF16)
        copies[2 * i + 2].wait()
        for s in range(segs):
            states_s[i * segs + s] = dot(state_ref[s], scaled_ref[s], TN)
    for c, order in enumerate(orders):
        near_ref, away_ref = refs[2 * c:2 * c + 2]
        count = near_ref.shape[2]
        for rel in range(4):
            place = rows_of(c, order, rel, count)
            for i in range(2 * segs):
                (near_ref, away_ref)[rel // 2][rel % 2, i] = states_s[i, pl.ds(place, count)]


def quad_kernel(seg, heads, in_ref, cot_ref, sin_ref, sout_ref, cum_ref, quad_ref, write_ref, read_ref):
    _, length, width = in_ref.shape
    pairs = width // BLOCK
    per = heads // pairs
    cum = cum_ref[...]
    cum_col = jnp.transpose(cum)
    scores = dot(sin_ref[0], sout_ref[0], NT)
    lane = lax.broadcasted_iota(jnp.int32, (length, BLOCK), 1) // (BLOCK // per)
    masked_cot = []
    for h in range(heads):
        pair = cot_ref[0, :, (h // per) * BLOCK:(h // per + 1) * BLOCK]
        masked_cot.append(jnp.where(lane == h % per, pair, jnp.zeros_like(pair)))
    causal = (
        lax.broadcasted_iota(jnp.int32, (BLOCK, BLOCK), 1)
        >= lax.broadcasted_iota(jnp.int32, (BLOCK, BLOCK), 0)
    )
    for u in range(0, length, BLOCK):
        coupled = None
        quads = [None] * pairs
        for h in range(heads):
            g = h // per
            row = seg * heads + h
            spread = cum[row:row + 1, u:] - cum_col[u:u + BLOCK, row:row + 1]
            decay = jnp.exp(spread)
            near = jnp.where(causal, decay[:, :BLOCK], 0.0)
            decay = near if u + BLOCK == length else jnp.concatenate([near, decay[:, BLOCK:]], axis=1)
            weights = (decay * scores[u:u + BLOCK, u:]).astype(BF16)
            part = dot(weights, masked_cot[h][u:], NN)
            quads[g] = part if quads[g] is None else quads[g] + part
            products = dot(in_ref[0, u:u + BLOCK, g * BLOCK:(g + 1) * BLOCK], masked_cot[h][u:], NT)
            coupled = decay * products if coupled is None else coupled + decay * products
        for g in range(pairs):
            quad_ref[u:u + BLOCK, g * BLOCK:(g + 1) * BLOCK] = quads[g]
        coupled = coupled.astype(BF16)
        write_ref[u:u + BLOCK] = dot(coupled, sout_ref[0, u:], NN)
        back = dot(coupled, sin_ref[0, u:u + BLOCK], TN)
        if u == 0:
            read_ref[...] = back
        else:
            read_ref[u:] += back


def plan_kernel(step_count, parents_ref, slots_ref, near_ref, grand_ref, hold_ref, up_ref, far_ref,
                flag_ref, at_ref, owner_s, slot_s):
    width = near_ref.shape[2]
    group = near_ref.shape[0]
    segs = group // 4
    count = slots_ref.shape[0] // segs
    me = lax.axis_index("seg")

    def note(j, carry):
        seg = slots_ref[j]

        @pl.when(seg < PARENTS)
        def _():
            owner_s[seg] = j // segs
            slot_s[seg] = j % segs

        return carry

    lax.fori_loop(0, slots_ref.shape[0], note, 0)

    def put(ref, i, j, value):
        ref[i, j:j + 1] = jnp.broadcast_to(value.astype(F32), (1, width))

    ids, above, top = [], [], []
    for j in range(group):
        seg = slots_ref[jnp.bitwise_xor(me, j // segs) * segs + j % segs]
        up = parents_ref[seg]
        known = jnp.maximum(up, 0)
        ids.append(seg)
        above.append(up)
        top.append(jnp.where(up >= 0, parents_ref[known], -1))
        away = jnp.bitwise_xor(owner_s[known], me)
        low, mid = jnp.bitwise_and(away, 1), jnp.bitwise_and(jnp.right_shift(away, 1), 1)
        row = (mid * (count // 2) + low * (count // 4) + jnp.right_shift(away, 2)) * segs + slot_s[known]
        at_ref[j:j + 1] = jnp.broadcast_to(row.astype(jnp.int32), (1, width))
    for j in range(group):
        for p in range(PARENTS):
            put(near_ref, j, p, above[j] == p)
            put(grand_ref, j, p, top[j] == p)
            put(hold_ref, j, p, ids[j] == p)
        for i in range(group):
            put(up_ref, j, i, above[j] == ids[i])
            put(far_ref, j, i, top[j] == ids[i])
    for p in range(PARENTS):
        away = jnp.bitwise_xor(owner_s[p], me)
        for k in range(step_count):
            high = jnp.right_shift(away, 2 + k)
            put(flag_ref, k, p, high == 0)
            put(flag_ref, step_count + k, p, high == 1)


def parent_decays(at_ref, decay_refs):
    decays = jnp.concatenate([ref[...] for ref in decay_refs], axis=0)
    row = lax.broadcasted_iota(jnp.int32, decays.shape, 0)
    return [
        jnp.sum(jnp.where(row == at_ref[j:j + 1], decays, 0.0), axis=0, keepdims=True)
        for j in range(at_ref.shape[0])
    ]


def raw_states(order, near_ref, first_ref, second_ref, segs, count):
    ends, adjs = [None] * (4 * segs), [None] * (4 * segs)
    for place, device in enumerate((0, 1 << order[0], 1 << order[1], 3)):
        for s in range(segs):
            for kind, found in ((0, ends), (1, adjs)):
                i = kind * segs + s
                if place < 2:
                    value = (near_ref, first_ref)[place][0, i]
                else:
                    at = ((place - 2) * 2 * segs + i) * count
                    value = second_ref[at:at + count]
                found[device * segs + s] = value
    return ends, adjs


def cross_kernel(order, step, near_p, grand_p, hold_p, flag_ref, at_ref, mine_ref, tail_ref,
                 near_ref, first_ref, second_ref, *refs):
    later, out_ref = refs[:-1], refs[-1]
    group = near_p.shape[0]
    segs = group // 4
    count = out_ref.shape[1]
    steps = flag_ref.shape[0] // 2
    decay = parent_decays(at_ref, (mine_ref, tail_ref))
    ends, adjs = raw_states(order, near_ref, first_ref, second_ref, segs, count)
    as_end = flag_ref[step]
    from_end = [as_end * hold_p[j] for j in range(group)]
    from_adj = [(1.0 - as_end) * (near_p[j] + grand_p[j] * decay[j]) for j in range(group)]
    passed = [
        jnp.where((as_end < 0.5) | (flag_ref[steps + j] > 0.5), 1.0, 0.0) for j in range(len(later))
    ]
    for p in range(PARENTS):
        value = 0.0
        for j in range(group):
            value += from_end[j][p:p + 1] * ends[j] + from_adj[j][p:p + 1] * adjs[j]
        for flag, got in zip(passed, later):
            value += flag[p:p + 1] * got[p]
        out_ref[p] = value


def finish_kernel(order, near_p, grand_p, hold_p, up_ref, far_ref, flag_ref, at_ref, mine_ref, tail_ref,
                  near_ref, first_ref, second_ref, *refs):
    later, (own_ref, there_ref, away_ref) = refs[:-3], refs[-3:]
    group = near_p.shape[0]
    segs = group // 4
    count = own_ref.shape[1]
    steps = flag_ref.shape[0] // 2
    decay = parent_decays(at_ref, (mine_ref, tail_ref))
    ends, adjs = raw_states(order, near_ref, first_ref, second_ref, segs, count)
    values, known = [], []
    for p in range(PARENTS):
        value, end = 0.0, 0.0
        for j, got in enumerate(later):
            value += got[p]
            end += flag_ref[steps + j, p:p + 1] * got[p]
        values.append(value)
        known.append(end)
    link = [up_ref[j] + far_ref[j] * decay[j] for j in range(group)]
    for place, device in enumerate((0, 1 << order[0], 1 << order[1], 3)):
        out_ref, base = ((own_ref, 0), (there_ref, 0), (away_ref, 0), (away_ref, 2 * segs))[place]
        for s in range(segs):
            j = device * segs + s
            weight = near_p[j] + grand_p[j] * decay[j]
            start, adj = 0.0, 0.0
            for i in range(group):
                start += link[j][i:i + 1] * ends[i]
                adj += link[i][j:j + 1] * adjs[i]
            for p in range(PARENTS):
                start += weight[p:p + 1] * known[p]
                adj += hold_p[j, p:p + 1] * values[p]
            out_ref[base + s] = start
            out_ref[base + segs + s] = adj


def state_kernel(orders, scin_ref, sccot_ref, *refs):
    parts, refs = refs[:3 * len(orders)], refs[3 * len(orders):]
    segs = scin_ref.shape[0]
    quads, refs = refs[:2 * segs], refs[2 * segs:]
    keep_w, send_w, keep_r, send_r, adj_out, start_s, total_s = refs
    for c, order in enumerate(orders):
        own, fourth, fifth = parts[3 * c:3 * c + 3]
        count = own.shape[1]
        for rel, (ref, base) in enumerate(((own, 0), (fourth, 0), (fifth, 0), (fifth, 2 * segs))):
            place = rows_of(c, order, rel, count)
            for s in range(segs):
                start_s[s, pl.ds(place, count)] = ref[base + s].astype(BF16)
                adj_out[s, pl.ds(place, count)] = ref[base + segs + s].astype(BF16)
    bit = lax.axis_index("head") % 2
    piece = keep_w.shape[2]
    for a, (scaled, table, keep_ref, send_ref) in enumerate(
        ((scin_ref, adj_out, keep_w, send_w), (sccot_ref, start_s, keep_r, send_r))
    ):
        for s in range(segs):
            total_s[a, s] = quads[2 * s + a][...] + dot(scaled[s], table[s], NT)
            for x in range(2):
                mine = pl.multiple_of((2 * x + bit) * piece, piece)
                other = pl.multiple_of((2 * x + 1 - bit) * piece, piece)
                keep_ref[x, s] = total_s[a, s, pl.ds(mine, piece)]
                send_ref[x, s] = total_s[a, s, pl.ds(other, piece)]


def inputs_kernel(sin_ref, toend_ref, adj_ref, *refs):
    quads, gin_ref = refs[:-1], refs[-1]
    segs, _, width = gin_ref.shape
    rows = toend_ref.shape[0] // 2
    for s in range(segs):
        to_end = dot(toend_ref[...], head_columns(rows, s, rows // segs, width), TN)
        gin_ref[s] = (quads[s][...] + to_end * dot(sin_ref[s], adj_ref[s], NN)).astype(BF16)


def whole(*shape):
    return pl.BlockSpec(shape, lambda *_: (0,) * len(shape))


def in_vmem():
    return pl.BlockSpec(memory_space=pltpu.VMEM)


def in_smem():
    return pl.BlockSpec(memory_space=pltpu.SMEM)


def flip(x, axis, count, bit):
    return lax.ppermute(x, axis, [(i, i ^ (1 << bit)) for i in range(count)])


PARAMS = pltpu.CompilerParams(vmem_limit_bytes=48 * 1024 * 1024)


def close_decays(decays, count):
    bits = count.bit_length() - 1
    if bits == 3:
        other, across, both = (
            lax.ppermute(decays, "seg", [(i, i ^ k) for i in range(count)]) for k in (1, 4, 5)
        )
        return jnp.concatenate([decays, across, other, both], axis=0)
    for bit in range(2, bits):
        decays = jnp.concatenate([decays, flip(decays, "seg", count, bit)], axis=0)
    return jnp.concatenate([decays, flip(decays, "seg", count, 0)], axis=0)


def tree_chain(order, count, plan, decays, near, near_late, first, second):
    near_p, grand_p, hold_p, up, far, flags, at = plan
    shape = near.shape[1:]
    part = jax.ShapeDtypeStruct(shape, F32)
    later = []
    for k in range(2, len(order)):
        send = pl.pallas_call(
            functools.partial(cross_kernel, order, k - 2),
            out_shape=jax.ShapeDtypeStruct((PARENTS, *shape[1:]), F32),
            in_specs=[in_vmem()] * (10 + len(later)),
            out_specs=in_vmem(),
            compiler_params=PARAMS,
            cost_estimate=pl.CostEstimate(flops=2_000_000, bytes_accessed=500_000, transcendentals=0),
            name="across_step",
        )(near_p, grand_p, hold_p, flags, at, *decays, near, first, second, *later)
        later.append(flip(send, "seg", count, order[k]))
    own, there, away = pl.pallas_call(
        functools.partial(finish_kernel, order),
        out_shape=(part, part, jax.ShapeDtypeStruct((2 * shape[0], *shape[1:]), F32)),
        in_specs=[in_vmem()] * (12 + len(later)),
        out_specs=(in_vmem(), in_vmem(), in_vmem()),
        compiler_params=PARAMS,
        cost_estimate=pl.CostEstimate(flops=2_000_000, bytes_accessed=500_000, transcendentals=0),
        name="finish_part",
    )(near_p, grand_p, hold_p, up, far, flags, at, *decays, near_late, first, second, *later)
    fourth = flip(away, "seg", count, order[1])
    fifth = flip(jnp.concatenate([there, fourth[shape[0]:]], axis=0), "seg", count, order[0])
    return own, fourth, fifth


def shards(mesh_sizes, inputs, cotangent, state_in, state_out, log_decay, parents, slot_segment):
    count = mesh_sizes["seg"]
    head_devices = mesh_sizes["head"]
    bit_count = count.bit_length() - 1
    segs, length, width = inputs.shape
    heads = log_decay.shape[1]
    state = state_in.shape[2]
    rows = segs * heads
    orders = [[0, 1] + list(range(2, bit_count)), [1, 0] + list(range(2, bit_count))]
    part_rows = state // (4 * len(orders))

    whole_in = whole(segs, length, width)
    whole_state = whole(segs, length, state)
    scaled = jax.ShapeDtypeStruct((segs, length, width), BF16)
    raw = jax.ShapeDtypeStruct((2, 2 * segs, part_rows, width), F32)
    scaled_in, scaled_cot, cum, to_end, decays, *raws = pl.pallas_call(
        functools.partial(local_kernel, orders),
        out_shape=(
            scaled, scaled,
            jax.ShapeDtypeStruct((rows, length), F32),
            jax.ShapeDtypeStruct((2 * rows, length), BF16),
            jax.ShapeDtypeStruct((segs, width), F32),
            *[raw] * (2 * len(orders)),
        ),
        in_specs=[pl.BlockSpec(memory_space=pltpu.HBM)] * 5,
        out_specs=tuple([in_vmem()] * (5 + 2 * len(orders))),
        scratch_shapes=[
            pltpu.VMEM((2 * segs, state, width), F32),
            pltpu.VMEM(inputs.shape, BF16),
            pltpu.VMEM(inputs.shape, BF16),
            pltpu.VMEM(state_in.shape, BF16),
            pltpu.VMEM(state_in.shape, BF16),
            pltpu.VMEM(log_decay.shape, F32),
            pltpu.SemaphoreType.DMA((5,)),
        ],
        compiler_params=PARAMS,
        cost_estimate=pl.CostEstimate(flops=200_000_000, bytes_accessed=4_000_000, transcendentals=8192),
        name="local_states",
    )(inputs, cotangent, state_in, state_out, log_decay)
    nears, aways = raws[0::2], raws[1::2]

    quads = []
    for s in range(segs):
        pick = lambda *_, s=s: (s, 0, 0)
        quads.append(
            pl.pallas_call(
                functools.partial(quad_kernel, s, heads),
                grid=(1,),
                out_shape=(
                    jax.ShapeDtypeStruct((length, width), F32),
                    jax.ShapeDtypeStruct((length, state), F32),
                    jax.ShapeDtypeStruct((length, state), F32),
                ),
                in_specs=[
                    pl.BlockSpec((1, length, width), pick),
                    pl.BlockSpec((1, length, width), pick),
                    pl.BlockSpec((1, length, state), pick),
                    pl.BlockSpec((1, length, state), pick),
                    whole(rows, length),
                ],
                out_specs=(whole(length, width), whole(length, state), whole(length, state)),
                compiler_params=PARAMS,
                cost_estimate=pl.CostEstimate(
                    flops=4_000_000_000, bytes_accessed=2_000_000, transcendentals=heads * length * length
                ),
                name="quadratic_part",
            )(inputs, cotangent, state_in, state_out, cum)
        )

    firsts = [flip(away, "seg", count, order[0]) for away, order in zip(aways, orders)]
    mine = close_decays(decays, count)
    held, quads[0] = lax.optimization_barrier((nears[0], quads[0]))
    late, quads[1:] = lax.optimization_barrier((nears[0], quads[1:]))
    raw_rows = 2 * segs * part_rows
    seconds = []
    for c, order in enumerate(orders):
        message = [(held if c == 0 else nears[c])[1].reshape(raw_rows, width), firsts[c][1].reshape(raw_rows, width)]
        if c == 0:
            message.append(mine)
        seconds.append(flip(jnp.concatenate(message, axis=0), "seg", count, order[1]))
    decays = (mine, seconds[0][2 * raw_rows:])

    group = 4 * segs
    by_parent = jax.ShapeDtypeStruct((group, PARENTS, width), F32)
    by_segment = jax.ShapeDtypeStruct((group, group, width), F32)
    plan = pl.pallas_call(
        functools.partial(plan_kernel, bit_count - 2),
        out_shape=(
            by_parent, by_parent, by_parent, by_segment, by_segment,
            jax.ShapeDtypeStruct((2 * (bit_count - 2), PARENTS, width), F32),
            jax.ShapeDtypeStruct((group, width), jnp.int32),
        ),
        in_specs=[in_smem(), in_smem()],
        out_specs=tuple([in_vmem()] * 7),
        scratch_shapes=[pltpu.SMEM((PARENTS,), jnp.int32), pltpu.SMEM((PARENTS,), jnp.int32)],
        compiler_params=PARAMS,
        cost_estimate=pl.CostEstimate(flops=2_000_000, bytes_accessed=500_000, transcendentals=0),
        name="plan_tree",
    )(parents, slot_segment)

    parts = []
    for c, order in enumerate(orders):
        last = late if c == 0 else nears[c]
        parts.extend(tree_chain(order, count, plan, decays, nears[c], last, firsts[c], seconds[c]))

    piece = length // head_devices
    half = jax.ShapeDtypeStruct((2, segs, piece, state), F32)
    keep_w, send_w, keep_r, send_r, adj_all = pl.pallas_call(
        functools.partial(state_kernel, orders),
        out_shape=(half, half, half, half, jax.ShapeDtypeStruct((segs, state, width), BF16)),
        in_specs=[in_vmem()] * (2 + len(parts) + 2 * segs),
        out_specs=tuple([in_vmem()] * 5),
        scratch_shapes=[
            pltpu.VMEM((segs, state, width), BF16),
            pltpu.VMEM((2, segs, length, state), F32),
        ],
        compiler_params=PARAMS,
        cost_estimate=pl.CostEstimate(flops=200_000_000, bytes_accessed=8_000_000, transcendentals=0),
        name="state_terms",
    )(scaled_in, scaled_cot, *parts, *[part for quad in quads for part in quad[1:]])

    grad_inputs = pl.pallas_call(
        inputs_kernel,
        out_shape=scaled,
        in_specs=[in_vmem()] * (3 + segs),
        out_specs=in_vmem(),
        compiler_params=PARAMS,
        cost_estimate=pl.CostEstimate(flops=200_000_000, bytes_accessed=8_000_000, transcendentals=0),
        name="grad_inputs",
    )(state_in, to_end, adj_all, *[quad[0] for quad in quads])

    place = lax.axis_index("head") // 2
    outs = []
    for keep, send in ((keep_w, send_w), (keep_r, send_r)):
        both = keep + flip(send, "head", head_devices, 0)
        away = lax.dynamic_index_in_dim(both, 1 - place, axis=0, keepdims=False)
        here = lax.dynamic_index_in_dim(both, place, axis=0, keepdims=False)
        outs.append(here + flip(away, "head", head_devices, 1))
    return grad_inputs, outs[0], outs[1]


def solution(mesh):
    sizes = {name: int(mesh.shape[name]) for name in ("seg", "head")}
    placed = (
        P("seg", None, "head"),
        P("seg", None, "head"),
        P("seg", None, None),
        P("seg", None, None),
        P("seg", "head", None),
        P(),
        P(),
    )
    return jax.shard_map(
        functools.partial(shards, sizes),
        mesh=mesh,
        in_specs=placed,
        out_specs=(P("seg", None, "head"), P("seg", "head", None), P("seg", "head", None)),
        check_vma=False,
    )
```

```python
import functools

import jax
import jax.numpy as jnp
from jax import lax
from jax.experimental import pallas as pl
from jax.experimental.pallas import tpu as pltpu
from jax.sharding import PartitionSpec as P

ROOTS = 2
MIDS = 6
PARENTS = ROOTS + MIDS
BLOCK = 128
TILE = 8
LOCAL_VMEM = 60 * 1024 * 1024
F32 = jnp.float32
BF16 = jnp.bfloat16


def dot(a, b, dims):
    return lax.dot_general(a, b, (dims, ((), ())), preferred_element_type=F32)


NN = ((1,), (0,))
NT = ((1,), (1,))
TN = ((0,), (0,))


def two_parts(x):
    upper = x.astype(BF16).astype(F32)
    return jnp.concatenate([upper, x - upper], axis=0).astype(BF16)


def head_columns(rows, seg, heads, width):
    row = lax.broadcasted_iota(jnp.int32, (2 * rows, width), 0) % rows
    col = lax.broadcasted_iota(jnp.int32, (2 * rows, width), 1) // (width // heads)
    return (row == seg * heads + col).astype(BF16)


def quarter_of(distance, count):
    place = jnp.bitwise_and(jnp.bitwise_xor(lax.axis_index("seg"), distance), 3)
    return pl.multiple_of(place * count, count)


def local_kernel(in_hbm, cot_hbm, sin_hbm, sout_hbm, decay_hbm,
                 scin_ref, sccot_ref, cum_ref, toend_ref, *refs):
    states_s, in_ref, cot_ref, sin_ref, sout_ref, decay_ref, sems = refs[-7:]
    copies = [
        pltpu.make_async_copy(src, dst, sems.at[i])
        for i, (src, dst) in enumerate((
            (decay_hbm, decay_ref), (in_hbm, in_ref), (sin_hbm, sin_ref),
            (cot_hbm, cot_ref), (sout_hbm, sout_ref),
        ))
    ]
    for copy in copies:
        copy.start()
    segs, _, width = in_ref.shape
    heads, length = decay_ref.shape[1:]
    rows = segs * heads
    copies[0].wait()
    decay = jnp.concatenate([decay_ref[s] for s in range(segs)], axis=0)
    p0 = decay.astype(BF16).astype(F32)
    r0 = decay - p0
    p1 = r0.astype(BF16).astype(F32)
    pieces = jnp.concatenate([p0, p1, r0 - p1], axis=0).astype(BF16)
    tri = (
        lax.broadcasted_iota(jnp.int32, (BLOCK, BLOCK), 0)
        <= lax.broadcasted_iota(jnp.int32, (BLOCK, BLOCK), 1)
    ).astype(BF16)
    before = jnp.zeros((rows, 1), F32)
    parts = []
    for b in range(length // BLOCK):
        sums = dot(pieces[:, b * BLOCK:(b + 1) * BLOCK], tri, NN)
        part = sums[:rows] + sums[rows:2 * rows] + sums[2 * rows:] + before
        before = part[:, BLOCK - 1:]
        parts.append(part)
    cum = jnp.concatenate(parts, axis=1)
    cum_ref[...] = cum
    row = lax.broadcasted_iota(jnp.int32, (rows, width), 0)
    col = lax.broadcasted_iota(jnp.int32, (rows, width), 1) // (width // heads)
    tail = refs[0].shape[0] - TILE
    for s in range(segs):
        of_head = jnp.where(row == s * heads + col, jnp.exp(before), 0.0)
        of_head = jnp.sum(of_head, axis=0, keepdims=True)
        for ref in refs[:4]:
            ref[tail + s:tail + s + 1] = of_head
    for ref in refs[:4]:
        ref[tail + segs:] = jnp.zeros((TILE - segs, width), F32)
    to_end = two_parts(jnp.exp(before - cum))
    toend_ref[...] = to_end
    from_start = two_parts(jnp.exp(cum))
    for i, (src, scaled_ref, factor, state_ref) in enumerate((
        (in_ref, scin_ref, to_end, sin_ref), (cot_ref, sccot_ref, from_start, sout_ref)
    )):
        copies[2 * i + 1].wait()
        for s in range(segs):
            spread = dot(factor, head_columns(rows, s, heads, width), TN)
            scaled_ref[s] = (src[s].astype(F32) * spread).astype(BF16)
        copies[2 * i + 2].wait()
        for s in range(segs):
            states_s[i * segs + s] = dot(state_ref[s], scaled_ref[s], TN)
    count = states_s.shape[1] // 4
    for distance, ref in enumerate(refs[:4]):
        place = quarter_of(distance, count)
        for i in range(2 * segs):
            ref[i * count:(i + 1) * count] = states_s[i, pl.ds(place, count)]


def quad_kernel(seg, heads, in_ref, cot_ref, sin_ref, sout_ref, cum_ref, quad_ref, write_ref, read_ref):
    _, length, width = in_ref.shape
    pairs = width // BLOCK
    per = heads // pairs
    cum = cum_ref[...]
    cum_col = jnp.transpose(cum)
    scores = dot(sin_ref[0], sout_ref[0], NT)
    lane = lax.broadcasted_iota(jnp.int32, (length, BLOCK), 1) // (BLOCK // per)
    masked_cot = []
    for h in range(heads):
        pair = cot_ref[0, :, (h // per) * BLOCK:(h // per + 1) * BLOCK]
        masked_cot.append(jnp.where(lane == h % per, pair, jnp.zeros_like(pair)))
    causal = (
        lax.broadcasted_iota(jnp.int32, (BLOCK, BLOCK), 1)
        >= lax.broadcasted_iota(jnp.int32, (BLOCK, BLOCK), 0)
    )
    for u in range(0, length, BLOCK):
        coupled = None
        quads = [None] * pairs
        for h in range(heads):
            g = h // per
            row = seg * heads + h
            spread = cum[row:row + 1, u:] - cum_col[u:u + BLOCK, row:row + 1]
            decay = jnp.exp(spread)
            near = jnp.where(causal, decay[:, :BLOCK], 0.0)
            decay = near if u + BLOCK == length else jnp.concatenate([near, decay[:, BLOCK:]], axis=1)
            weights = (decay * scores[u:u + BLOCK, u:]).astype(BF16)
            part = dot(weights, masked_cot[h][u:], NN)
            quads[g] = part if quads[g] is None else quads[g] + part
            products = dot(in_ref[0, u:u + BLOCK, g * BLOCK:(g + 1) * BLOCK], masked_cot[h][u:], NT)
            coupled = decay * products if coupled is None else coupled + decay * products
        for g in range(pairs):
            quad_ref[u:u + BLOCK, g * BLOCK:(g + 1) * BLOCK] = quads[g]
        coupled = coupled.astype(BF16)
        write_ref[u:u + BLOCK] = dot(coupled, sout_ref[0, u:], NN)
        back = dot(coupled, sin_ref[0, u:u + BLOCK], TN)
        if u == 0:
            read_ref[...] = back
        else:
            read_ref[u:] += back


def plan_kernel(step_count, parents_ref, slots_ref, near_ref, grand_ref, hold_ref, up_ref, far_ref,
                flag_ref, at_ref, owner_s, slot_s):
    width = near_ref.shape[2]
    group = near_ref.shape[0]
    segs = group // 4
    me = lax.axis_index("seg")

    def note(j, carry):
        seg = slots_ref[j]

        @pl.when(seg < PARENTS)
        def _():
            owner_s[seg] = j // segs
            slot_s[seg] = j % segs

        return carry

    lax.fori_loop(0, slots_ref.shape[0], note, 0)

    def put(ref, i, j, value):
        ref[i, j:j + 1] = jnp.broadcast_to(value.astype(F32), (1, width))

    ids, above, top = [], [], []
    for j in range(group):
        seg = slots_ref[jnp.bitwise_xor(me, j // segs) * segs + j % segs]
        up = parents_ref[seg]
        known = jnp.maximum(up, 0)
        ids.append(seg)
        above.append(up)
        top.append(jnp.where(up >= 0, parents_ref[known], -1))
        away = jnp.bitwise_xor(owner_s[known], me)
        row = away * segs + slot_s[known]
        at_ref[j:j + 1] = jnp.broadcast_to(row.astype(jnp.int32), (1, width))
    for j in range(group):
        for p in range(PARENTS):
            put(near_ref, j, p, above[j] == p)
            put(grand_ref, j, p, top[j] == p)
            put(hold_ref, j, p, ids[j] == p)
        for i in range(group):
            put(up_ref, j, i, above[j] == ids[i])
            put(far_ref, j, i, top[j] == ids[i])
    for p in range(PARENTS):
        away = jnp.bitwise_xor(owner_s[p], me)
        for k in range(step_count):
            high = jnp.right_shift(away, 2 + k)
            put(flag_ref, k, p, high == 0)
            put(flag_ref, step_count + k, p, high == 1)


def group_decays(raws, into, at, segs):
    tail = raws[0].shape[0] - TILE
    for place, ref in enumerate(raws):
        into[at + place * segs:at + (place + 1) * segs] = ref[tail:tail + segs]


def parent_decays(at_ref, decays):
    row = lax.broadcasted_iota(jnp.int32, decays.shape, 0)
    return [
        jnp.sum(jnp.where(row == at_ref[j:j + 1], decays, 0.0), axis=0, keepdims=True)
        for j in range(at_ref.shape[0])
    ]


def raw_states(raws, segs, count):
    ends = [ref[s * count:(s + 1) * count] for ref in raws for s in range(segs)]
    adjs = [ref[(segs + s) * count:(segs + s + 1) * count] for ref in raws for s in range(segs)]
    return ends, adjs


def cross_kernel(step, carried, near_p, grand_p, hold_p, flag_ref, at_ref, *refs):
    raws, later, out_ref = refs[:4], refs[4:-1], refs[-1]
    group = near_p.shape[0]
    segs = group // 4
    count = out_ref.shape[0] // (PARENTS * TILE) * TILE
    steps = flag_ref.shape[0] // 2
    if carried:
        group_decays(raws, out_ref, PARENTS * count, segs)
        decay = parent_decays(at_ref, out_ref[PARENTS * count:PARENTS * count + group])
    else:
        decay = parent_decays(at_ref, later[0][...])
        later = later[1:]
    ends, adjs = raw_states(raws, segs, count)
    as_end = flag_ref[step]
    from_end = [as_end * hold_p[j] for j in range(group)]
    from_adj = [(1.0 - as_end) * (near_p[j] + grand_p[j] * decay[j]) for j in range(group)]
    passed = [
        jnp.where((as_end < 0.5) | (flag_ref[steps + j] > 0.5), 1.0, 0.0) for j in range(len(later))
    ]
    for p in range(PARENTS):
        value = 0.0
        for j in range(group):
            value += from_end[j][p:p + 1] * ends[j] + from_adj[j][p:p + 1] * adjs[j]
        for flag, got in zip(passed, later):
            value += flag[p:p + 1] * got[p * count:(p + 1) * count]
        out_ref[p * count:(p + 1) * count] = value


def finish_kernel(carried, near_p, grand_p, hold_p, up_ref, far_ref, flag_ref, at_ref, *refs):
    raws, refs = refs[:4], refs[4:]
    outs, decays_s = refs[-5:-1], refs[-1]
    later = refs[:-5]
    group = near_p.shape[0]
    segs = group // 4
    count = outs[0].shape[0] // (2 * segs)
    steps = flag_ref.shape[0] // 2
    if carried:
        group_decays(raws, decays_s, 0, segs)
        decays_s[group:] = later[0][PARENTS * count:PARENTS * count + group]
        decay = parent_decays(at_ref, decays_s[...])
    else:
        decay = parent_decays(at_ref, later[0][...])
        later = later[1:]
    ends, adjs = raw_states(raws, segs, count)
    values, known = [], []
    for p in range(PARENTS):
        value, end = 0.0, 0.0
        for j, got in enumerate(later):
            part = got[p * count:(p + 1) * count]
            value += part
            end += flag_ref[steps + j, p:p + 1] * part
        values.append(value)
        known.append(end)
    link = [up_ref[j] + far_ref[j] * decay[j] for j in range(group)]
    for j in range(group):
        weight = near_p[j] + grand_p[j] * decay[j]
        takes = hold_p[j]
        if carried:
            for i in range(group):
                takes += (up_ref[i, j:j + 1] * decays_s[i:i + 1]) * hold_p[i]
        start, adj = 0.0, 0.0
        for i in range(group):
            start += link[j][i:i + 1] * ends[i]
            adj += link[i][j:j + 1] * adjs[i]
        for p in range(PARENTS):
            start += weight[p:p + 1] * known[p]
            adj += takes[p:p + 1] * values[p]
        out_ref, s = outs[j // segs], j % segs
        out_ref[s * count:(s + 1) * count] = start
        out_ref[(segs + s) * count:(segs + s + 1) * count] = adj


def state_kernel(scin_ref, sccot_ref, *refs):
    parts, refs = refs[:4], refs[4:]
    segs = scin_ref.shape[0]
    quads, refs = refs[:2 * segs], refs[2 * segs:]
    keep_w, send_w, keep_r, send_r, adj_out, start_s, total_s = refs
    count = parts[0].shape[0] // (2 * segs)
    for distance, ref in enumerate(parts):
        place = quarter_of(distance, count)
        for s in range(segs):
            start_s[s, pl.ds(place, count)] = ref[s * count:(s + 1) * count].astype(BF16)
            adj_out[s, pl.ds(place, count)] = ref[(segs + s) * count:(segs + s + 1) * count].astype(BF16)
    bit = lax.axis_index("head") % 2
    piece = keep_w.shape[2]
    for a, (scaled, table, keep_ref, send_ref) in enumerate(
        ((scin_ref, adj_out, keep_w, send_w), (sccot_ref, start_s, keep_r, send_r))
    ):
        for s in range(segs):
            total_s[a, s] = quads[2 * s + a][...] + dot(scaled[s], table[s], NT)
            for x in range(2):
                mine = pl.multiple_of((2 * x + bit) * piece, piece)
                other = pl.multiple_of((2 * x + 1 - bit) * piece, piece)
                keep_ref[x, s] = total_s[a, s, pl.ds(mine, piece)]
                send_ref[x, s] = total_s[a, s, pl.ds(other, piece)]


def inputs_kernel(sin_ref, toend_ref, adj_ref, *refs):
    quads, gin_ref = refs[:-1], refs[-1]
    segs, _, width = gin_ref.shape
    rows = toend_ref.shape[0] // 2
    for s in range(segs):
        to_end = dot(toend_ref[...], head_columns(rows, s, rows // segs, width), TN)
        gin_ref[s] = (quads[s][...] + to_end * dot(sin_ref[s], adj_ref[s], NN)).astype(BF16)


def whole(*shape):
    return pl.BlockSpec(shape, lambda *_: (0,) * len(shape))


def in_vmem():
    return pl.BlockSpec(memory_space=pltpu.VMEM)


def in_smem():
    return pl.BlockSpec(memory_space=pltpu.SMEM)


def flip(x, axis, count, bit):
    return lax.ppermute(x, axis, [(i, i ^ (1 << bit)) for i in range(count)])


PARAMS = pltpu.CompilerParams(vmem_limit_bytes=48 * 1024 * 1024)


def to_distance(x, count, distance):
    return lax.ppermute(x, "seg", [(i, i ^ distance) for i in range(count)])


def shards(mesh_sizes, inputs, cotangent, state_in, state_out, log_decay, parents, slot_segment):
    count = mesh_sizes["seg"]
    head_devices = mesh_sizes["head"]
    bit_count = count.bit_length() - 1
    segs, length, width = inputs.shape
    heads = log_decay.shape[1]
    state = state_in.shape[2]
    rows = segs * heads
    quarter = state // 4
    group = 4 * segs
    steps = bit_count - 2

    scaled = jax.ShapeDtypeStruct((segs, length, width), BF16)
    raw = jax.ShapeDtypeStruct((2 * segs * quarter + TILE, width), F32)
    scaled_in, scaled_cot, cum, to_end, *raws = pl.pallas_call(
        local_kernel,
        out_shape=(
            scaled, scaled,
            jax.ShapeDtypeStruct((rows, length), F32),
            jax.ShapeDtypeStruct((2 * rows, length), BF16),
            *[raw] * 4,
        ),
        in_specs=[pl.BlockSpec(memory_space=pltpu.HBM)] * 5,
        out_specs=tuple([in_vmem()] * 8),
        scratch_shapes=[
            pltpu.VMEM((2 * segs, state, width), F32),
            pltpu.VMEM(inputs.shape, BF16),
            pltpu.VMEM(inputs.shape, BF16),
            pltpu.VMEM(state_in.shape, BF16),
            pltpu.VMEM(state_in.shape, BF16),
            pltpu.VMEM(log_decay.shape, F32),
            pltpu.SemaphoreType.DMA((5,)),
        ],
        compiler_params=pltpu.CompilerParams(vmem_limit_bytes=LOCAL_VMEM),
        cost_estimate=pl.CostEstimate(flops=200_000_000, bytes_accessed=4_000_000, transcendentals=8192),
        name="local_states",
    )(inputs, cotangent, state_in, state_out, log_decay)

    group_raws = [raws[0]] + [to_distance(raws[d], count, d) for d in range(1, 4)]

    quads = []
    for s in range(segs):
        pick = lambda *_, s=s: (s, 0, 0)
        quads.append(
            pl.pallas_call(
                functools.partial(quad_kernel, s, heads),
                grid=(1,),
                out_shape=(
                    jax.ShapeDtypeStruct((length, width), F32),
                    jax.ShapeDtypeStruct((length, state), F32),
                    jax.ShapeDtypeStruct((length, state), F32),
                ),
                in_specs=[
                    pl.BlockSpec((1, length, width), pick),
                    pl.BlockSpec((1, length, width), pick),
                    pl.BlockSpec((1, length, state), pick),
                    pl.BlockSpec((1, length, state), pick),
                    whole(rows, length),
                ],
                out_specs=(whole(length, width), whole(length, state), whole(length, state)),
                compiler_params=PARAMS,
                cost_estimate=pl.CostEstimate(
                    flops=4_000_000_000, bytes_accessed=2_000_000, transcendentals=heads * length * length
                ),
                name="quadratic_part",
            )(inputs, cotangent, state_in, state_out, cum)
        )

    by_parent = jax.ShapeDtypeStruct((group, PARENTS, width), F32)
    by_segment = jax.ShapeDtypeStruct((group, group, width), F32)
    plan = pl.pallas_call(
        functools.partial(plan_kernel, steps),
        out_shape=(
            by_parent, by_parent, by_parent, by_segment, by_segment,
            jax.ShapeDtypeStruct((2 * steps, PARENTS, width), F32),
            jax.ShapeDtypeStruct((group, width), jnp.int32),
        ),
        in_specs=[in_smem(), in_smem()],
        out_specs=tuple([in_vmem()] * 7),
        scratch_shapes=[pltpu.SMEM((PARENTS,), jnp.int32), pltpu.SMEM((PARENTS,), jnp.int32)],
        compiler_params=PARAMS,
        cost_estimate=pl.CostEstimate(flops=2_000_000, bytes_accessed=500_000, transcendentals=0),
        name="plan_tree",
    )(parents, slot_segment)

    own, quads[0] = lax.optimization_barrier((raws[0], quads[0]))
    own_late, quads[1:] = lax.optimization_barrier((raws[0], quads[1:]))
    near_p, grand_p, hold_p, up, far, flags, at = plan

    carried = steps == 1
    decays = []
    if not carried:
        known = raws[0][2 * segs * quarter:2 * segs * quarter + segs]
        for bit in range(bit_count):
            known = jnp.concatenate([known, to_distance(known, count, 1 << bit)], axis=0)
        decays = [known]
    later = []
    for k in range(steps):
        message = (PARENTS * quarter + (TILE if carried else 0), width)
        send = pl.pallas_call(
            functools.partial(cross_kernel, k, carried),
            out_shape=jax.ShapeDtypeStruct(message, F32),
            in_specs=[in_vmem()] * (9 + len(decays) + len(later)),
            out_specs=in_vmem(),
            compiler_params=PARAMS,
            cost_estimate=pl.CostEstimate(flops=2_000_000, bytes_accessed=500_000, transcendentals=0),
            name="across_step",
        )(near_p, grand_p, hold_p, flags, at, own, *group_raws[1:], *decays, *later)
        later.append(to_distance(send, count, 4 << k))

    part = jax.ShapeDtypeStruct((2 * segs * quarter, width), F32)
    parts = pl.pallas_call(
        functools.partial(finish_kernel, carried),
        out_shape=(part, part, part, part),
        in_specs=[in_vmem()] * (11 + len(decays) + len(later)),
        out_specs=tuple([in_vmem()] * 4),
        scratch_shapes=[pltpu.VMEM((2 * group, width), F32)],
        compiler_params=PARAMS,
        cost_estimate=pl.CostEstimate(flops=2_000_000, bytes_accessed=500_000, transcendentals=0),
        name="finish_states",
    )(near_p, grand_p, hold_p, up, far, flags, at, own_late, *group_raws[1:], *decays, *later)
    parts = [parts[0]] + [to_distance(parts[d], count, d) for d in range(1, 4)]

    piece = length // head_devices
    half = jax.ShapeDtypeStruct((2, segs, piece, state), F32)
    keep_w, send_w, keep_r, send_r, adj_all = pl.pallas_call(
        state_kernel,
        out_shape=(half, half, half, half, jax.ShapeDtypeStruct((segs, state, width), BF16)),
        in_specs=[in_vmem()] * (2 + len(parts) + 2 * segs),
        out_specs=tuple([in_vmem()] * 5),
        scratch_shapes=[
            pltpu.VMEM((segs, state, width), BF16),
            pltpu.VMEM((2, segs, length, state), F32),
        ],
        compiler_params=PARAMS,
        cost_estimate=pl.CostEstimate(flops=200_000_000, bytes_accessed=8_000_000, transcendentals=0),
        name="state_terms",
    )(scaled_in, scaled_cot, *parts, *[part for quad in quads for part in quad[1:]])

    grad_inputs = pl.pallas_call(
        inputs_kernel,
        out_shape=scaled,
        in_specs=[in_vmem()] * (3 + segs),
        out_specs=in_vmem(),
        compiler_params=PARAMS,
        cost_estimate=pl.CostEstimate(flops=200_000_000, bytes_accessed=8_000_000, transcendentals=0),
        name="grad_inputs",
    )(state_in, to_end, adj_all, *[quad[0] for quad in quads])

    place = lax.axis_index("head") // 2
    outs = []
    for keep, send in ((keep_w, send_w), (keep_r, send_r)):
        both = keep + flip(send, "head", head_devices, 0)
        away = lax.dynamic_index_in_dim(both, 1 - place, axis=0, keepdims=False)
        here = lax.dynamic_index_in_dim(both, place, axis=0, keepdims=False)
        outs.append(here + flip(away, "head", head_devices, 1))
    return grad_inputs, outs[0], outs[1]


def solution(mesh):
    sizes = {name: int(mesh.shape[name]) for name in ("seg", "head")}
    placed = (
        P("seg", None, "head"),
        P("seg", None, "head"),
        P("seg", None, None),
        P("seg", None, None),
        P("seg", "head", None),
        P(),
        P(),
    )
    return jax.shard_map(
        functools.partial(shards, sizes),
        mesh=mesh,
        in_specs=placed,
        out_specs=(P("seg", None, "head"), P("seg", "head", None), P("seg", "head", None)),
        check_vma=False,
    )
```
